32 devices in a mesh: grp: 2 (over y), clu: 4 (over z), arc: 4 (over x, core).
Axes of the slice: x: 2, y: 2, z: 4, core: 2. Of those that a mesh axis runs over, the one named last changes fastest.
Arguments:
- features: bfloat16 [8, 4, 16, 64, 128], P(('grp', 'clu'), 'arc'), parts along dimension 0, may hold values from -12 to 12
- cotangent: bfloat16 [8, 4, 16, 64, 128], P(('grp', 'clu'), 'arc'), parts along dimension 0, may hold values from -6 to 6
- w_out_att: bfloat16 [128, 384], replicated, may hold values from -0.5 to 0.5
- w_in_att: bfloat16 [128, 384], replicated, may hold values from -0.5 to 0.5
- w_mix: bfloat16 [256, 128], replicated, may hold values from -0.375 to 0.375
- in_degree: int32 [8, 4, 16], P(('grp', 'clu'), 'arc'), parts along dimension 0, may hold values from 1 to 128, 1024 in all within a row
- in_order: int32 [8, 4, 1024], P(('grp', 'clu'), 'arc'), parts along dimension 0, may hold values from 0 to 1023, each once within a row
Outputs:
- mixed: bfloat16 [8, 4, 16, 64, 128], P(('grp', 'clu'), 'arc'), parts along dimension 0
- feature_grad: bfloat16 [8, 4, 16, 64, 128], P(('grp', 'clu'), 'arc'), parts along dimension 0
The draws below stay inside these ranges and needn't reach their ends.
There are 2 independent parts, one for each index of `grp`. The reference program is written for one: setup_inputs(seed, part) draws one part's arguments, and reference() takes and returns one part's arrays. A program takes and returns all parts, laid end to end along the dimension named above; an argument that names none is the same for every part. Nothing has to cross between parts.
Inputs may be any that keep to these rules, and one draw needn't show every extreme that they name: `in_degree`: the in-degrees of each block's 16 cities sum to 1024; some city of every block has exactly 128. `in_order`: each block's row holds every number below 1024 once.
All inputs are finite; a program needn't handle non-finite values.
Results may differ from the reference program's by a relative error of at most 0.014.
The reference program's roundings to bfloat16 on the way count: a program that leaves them out, or rounds other values in their place, can miss the bound.
Values may be sent and summed in bfloat16 or wider, within the bound.
A program may use at most 64 MiB of HBM per device.

```python
import math
import jax
import jax.numpy as jnp
import numpy as np
from jax import lax

D = 128
HEADS = 8
K = 64
CROSS = 16
IN_MAX = 128
CITY_DEV = 16
ROWS = 1024
N_CLU = 4
N_ARC = 4


def draw_features(key, part):
    shape = (N_CLU, N_ARC, CITY_DEV, K, D)
    first_key = jax.random.fold_in(key, 0)
    values = jax.random.normal(first_key, shape, jnp.float32)
    return jnp.clip(values, -12.0, 12.0).astype(jnp.bfloat16)


def levels(key, shape, cuts, low, high):
    def one(dim, shards_of):
        heights = jax.random.uniform(jax.random.fold_in(jax.random.fold_in(key, 6), dim), (shards_of,), jnp.float32, low / len(cuts), high / len(cuts))
        return jnp.repeat(jnp.exp(heights), shape[dim] // shards_of).reshape((-1,) + (1,) * (len(shape) - dim - 1))

    gain = one(*cuts[0])
    for cut in cuts[1:]:
        gain = gain * one(*cut)
    return gain


def length_profile(amount, total, bound, lean):
    loads = [(1 << 20) // math.isqrt(standing ** lean) + 1 for standing in range(2, amount + 1)]
    surplus, holding = total - bound - (amount - 1), [1] * (amount - 1)
    while surplus > 0:
        candidates = [i for i in range(amount - 1) if holding[i] < bound]
        pool, remaining = sum([loads[i] for i in candidates]), surplus
        for i in candidates:
            extra = min(bound - holding[i], max(1, remaining * loads[i] // pool), surplus)
            holding[i] = holding[i] + extra
            surplus = surplus - extra
    return np.array([bound] + holding)


def ragged_sizes(key, count, total, bound, lean):
    if count == 2:
        one = jax.random.randint(key, (), max(1, total - bound), min(bound, total - 1) + 1)
        return jnp.stack([one, total - one])
    lengths = jnp.asarray(length_profile(count, total, bound, lean), jnp.int32)
    twos = (count - 1) // 2
    donor, receiver = lengths[1:1 + 2 * twos:2], lengths[2:2 + 2 * twos:2]
    margin = jnp.minimum(donor - 1, bound - receiver)
    shifted = jax.random.randint(jax.random.fold_in(key, 1), (twos,), 0, 1 << 20) % (margin + 1)
    lengths = lengths.at[1:1 + 2 * twos:2].set(donor - shifted).at[2:2 + 2 * twos:2].set(receiver + shifted)
    return lengths[jax.random.permutation(jax.random.fold_in(key, 2), count)]


def centred(key, extent, width, limit, cuts=(), held_as=jnp.bfloat16):
    values = width * jax.random.normal(key, extent, jnp.float32)
    if cuts:
        values = values * levels(key, extent, cuts, -0.22, 0.18)
    return jnp.clip(values, -limit, limit).astype(held_as)


def setup_inputs(seed: int = 0, part: int = 0) -> dict:
    seeds = jax.random.split(jax.random.key(seed), 8)
    part_splits = jax.random.split(jax.random.fold_in(seeds[7], part), 8)
    return {
        "features": draw_features(jax.random.fold_in(jax.random.fold_in(seeds[7], part), 71), part),
        "cotangent": centred(part_splits[1], (N_CLU, N_ARC, CITY_DEV, K, D), 1.0, 6.0, ((0, 4), (1, 4))),
        "w_out_att": centred(seeds[2], (D, 3 * D), D ** -0.5, 0.5),
        "w_in_att": centred(seeds[3], (D, 3 * D), D ** -0.5, 0.5),
        "w_mix": centred(seeds[4], (2 * D, D), (2 * D) ** -0.5, 0.375),
        "in_degree": jax.vmap(lambda own: ragged_sizes(own, CITY_DEV, ROWS, IN_MAX, 2))(jax.random.split(part_splits[5], N_CLU * N_ARC)).reshape((N_CLU, N_ARC, CITY_DEV)).astype(jnp.int32),
        "in_order": jax.vmap(lambda own: jax.random.permutation(own, ROWS))(jax.random.split(part_splits[6], N_CLU * N_ARC)).reshape((N_CLU, N_ARC, ROWS)).astype(jnp.int32),
    }


def split_heads(tensor):
    return tensor.reshape(tensor.shape[:-1] + (HEADS, tensor.shape[-1] // HEADS))

def attend(projected, live_slots):
    feature_width = projected.shape[-1] // 3
    queries = split_heads(projected[..., :feature_width]).astype(jnp.float32)
    key_rows = split_heads(projected[..., feature_width:2 * feature_width]).astype(jnp.float32)
    values = split_heads(projected[..., 2 * feature_width:]).astype(jnp.float32)
    scores = jnp.einsum('bqhd,bkhd->bhqk', queries, key_rows) * (1.0 / math.sqrt(feature_width // HEADS))
    if live_slots is not None:
        scores = jnp.where(live_slots[:, None, None, :], scores, -1e+30)
    highest = lax.optimization_barrier(jnp.max(scores, axis=-1, keepdims=True))
    raised = jnp.exp(scores - highest)
    weights = lax.optimization_barrier((raised / lax.optimization_barrier(jnp.sum(raised, axis=-1, keepdims=True))).astype(jnp.bfloat16))
    blended = jnp.einsum('bhqk,bkhd->bqhd', weights.astype(jnp.float32), values)
    return blended.reshape(projected.shape[:-1] + (feature_width,)).astype(jnp.bfloat16)

def to_targets(field):
    inner = K - CROSS
    per_peer = inner // N_ARC
    channels = field.shape[-1]
    inside = field[:, :, :, :inner].reshape(N_CLU, N_ARC, CITY_DEV, N_ARC, per_peer, channels)
    inside = inside.transpose(0, 3, 2, 1, 4, 5).reshape(N_CLU, N_ARC, CITY_DEV * inner, channels)
    onward = jnp.roll(field[:, :, :, inner:], 1, axis=0).reshape(N_CLU, N_ARC, CITY_DEV * CROSS, channels)
    return jnp.concatenate([inside, onward], axis=2)

def to_sources(grouped_rows):
    inner = K - CROSS
    per_peer = inner // N_ARC
    channels = grouped_rows.shape[-1]
    inside = grouped_rows[:, :, :CITY_DEV * inner].reshape(N_CLU, N_ARC, CITY_DEV, N_ARC, per_peer, channels)
    inside = inside.transpose(0, 3, 2, 1, 4, 5).reshape(N_CLU, N_ARC, CITY_DEV, inner, channels)
    onward = grouped_rows[:, :, CITY_DEV * inner:].reshape(N_CLU, N_ARC, CITY_DEV, CROSS, channels)
    onward = jnp.roll(onward, -1, axis=0)
    return jnp.concatenate([inside, onward], axis=3)

def target_layout(degree, row_count):
    offsets = (jnp.cumsum(degree) - degree).astype(jnp.int32)
    slot_ids = jnp.arange(IN_MAX, dtype=jnp.int32)
    slot_index = jnp.minimum(offsets[:, None] + slot_ids[None, :], row_count - 1).astype(jnp.int32)
    live_slots = slot_ids[None, :] < degree[:, None]
    positions = jnp.arange(row_count, dtype=jnp.int32)
    started = offsets[None, :] <= positions[:, None]
    owner_ids = (lax.optimization_barrier(jnp.sum(started.astype(jnp.int32), axis=1)) - 1).astype(jnp.int32)
    starts = lax.optimization_barrier(jnp.max(jnp.where(started, offsets[None, :], 0), axis=1)).astype(jnp.int32)
    flat_index = (owner_ids * IN_MAX + positions - starts).astype(jnp.int32)
    return (slot_index, live_slots, flat_index)

def in_forward_dev(grouped, degree):
    slot_index, live_slots, flat_index = target_layout(degree, grouped.shape[0])
    tile_rows = grouped[slot_index]
    blocks = tile_rows.reshape(-1, 8, IN_MAX, tile_rows.shape[-1])
    live_blocks = live_slots.reshape(-1, 8, IN_MAX)
    outcome = lax.map(lambda bundle: attend(bundle[0], bundle[1]), (blocks, live_blocks))
    return outcome.reshape(-1, outcome.shape[-1])[flat_index]

def out_pull(projected, grad_out):
    _, pull = jax.vjp(lambda operand: attend(operand, None), projected)
    return pull(grad_out)[0]

def in_pull(grouped, degree, grad_grouped):
    _, pull = jax.vjp(lambda operand: in_forward_dev(operand, degree), grouped)
    return pull(grad_grouped)[0]

def reference(features, cotangent, w_out_att, w_in_att, w_mix, in_degree, in_order):
    feature_width = features.shape[-1]
    block_count = N_CLU * N_ARC
    row_count = CITY_DEV * K
    flat_rows = features.reshape(-1, feature_width)
    proj_out = jnp.dot(flat_rows, w_out_att, preferred_element_type=jnp.float32).astype(jnp.bfloat16)
    proj_in = jnp.dot(flat_rows, w_in_att, preferred_element_type=jnp.float32).astype(jnp.bfloat16)
    proj_out_blocks = proj_out.reshape(block_count, CITY_DEV, K, 3 * feature_width)
    out_att = lax.map(lambda city_block: attend(city_block, None), proj_out_blocks)
    received = to_targets(proj_in.reshape(N_CLU, N_ARC, CITY_DEV, K, 3 * feature_width))
    target_order = in_order.reshape(block_count, row_count).astype(jnp.int32)
    degrees = in_degree.reshape(block_count, CITY_DEV).astype(jnp.int32)
    grouped = jnp.take_along_axis(received.reshape(block_count, row_count, 3 * feature_width), target_order[:, :, None], axis=1)
    in_grouped = lax.map(lambda bundle: in_forward_dev(bundle[0], bundle[1]), (grouped, degrees))
    inverse = jnp.argsort(target_order, axis=1).astype(jnp.int32)
    in_back = jnp.take_along_axis(in_grouped, inverse[:, :, None], axis=1)
    in_att = to_sources(in_back.reshape(N_CLU, N_ARC, row_count, feature_width))
    combined = jnp.concatenate([out_att.reshape(-1, feature_width), in_att.reshape(-1, feature_width)], axis=1)
    mixed = (flat_rows.astype(jnp.float32) + jnp.dot(combined, w_mix, preferred_element_type=jnp.float32)).astype(jnp.bfloat16)
    upstream = cotangent.reshape(-1, feature_width)
    mix_grad = jnp.dot(upstream, w_mix.T, preferred_element_type=jnp.float32).astype(jnp.bfloat16)
    d_out = mix_grad[:, :feature_width].reshape(block_count, CITY_DEV, K, feature_width)
    d_in = mix_grad[:, feature_width:].reshape(N_CLU, N_ARC, CITY_DEV, K, feature_width)
    d_proj_out = lax.map(lambda bundle: out_pull(bundle[0], bundle[1]), (proj_out_blocks, d_out))
    d_in_grouped = jnp.take_along_axis(to_targets(d_in).reshape(block_count, row_count, feature_width), target_order[:, :, None], axis=1)
    d_grouped = lax.map(lambda bundle: in_pull(bundle[0], bundle[1], bundle[2]), (grouped, degrees, d_in_grouped))
    d_back = jnp.take_along_axis(d_grouped, inverse[:, :, None], axis=1)
    d_home = to_sources(d_back.reshape(N_CLU, N_ARC, row_count, 3 * feature_width))
    in_grad = jnp.dot(d_home.reshape(-1, 3 * feature_width), w_in_att.T, preferred_element_type=jnp.float32).astype(jnp.bfloat16)
    in_grad = lax.optimization_barrier(in_grad).astype(jnp.float32)
    out_grad = jnp.dot(d_proj_out.reshape(-1, 3 * feature_width), w_out_att.T, preferred_element_type=jnp.float32)
    feature_grad = (upstream.astype(jnp.float32) + out_grad + in_grad).astype(jnp.bfloat16)
    return (mixed.reshape(features.shape), feature_grad.reshape(features.shape))
```

```python
import functools

import jax
import jax.numpy as jnp
from jax import lax
from jax.experimental import pallas as pl
from jax.experimental.pallas import tpu as pltpu
from jax.sharding import PartitionSpec as P

HEADS = 8
K = 64
CROSS = 16
IN_MAX = 128
INNER = K - CROSS
MESH = pl.DeviceIdType.MESH
F32 = jnp.float32
BF = jnp.bfloat16


def mm(a, b):
    return lax.dot_general(a, b, (((1,), (0,)), ((), ())), preferred_element_type=F32)


def mt(a, b):
    return lax.dot_general(a, b, (((1,), (1,)), ((), ())), preferred_element_type=F32)


def iota(shape, dim):
    return lax.broadcasted_iota(jnp.int32, shape, dim).astype(F32)


def fdiv(x, c):
    return jnp.floor((x + 0.5) * (1.0 / c))


def onehot(a, b):
    return jnp.where(a == b, 1.0, 0.0).astype(BF)


def head_masks(width):
    lane = lax.broadcasted_iota(jnp.int32, (16, width), 1)
    size = width // HEADS
    return [
        jnp.where((lane >= h * size) & (lane < (h + 1) * size), 1.0, 0.0).astype(BF)[0:1]
        for h in range(HEADS)
    ]


def attend(proj, d_out, bias, masks):
    width = d_out.shape[1]
    size = width // HEADS
    scale = size ** -0.5
    queries = (proj[:, :width] * scale).astype(BF)
    keys = proj[:, width : 2 * width]
    values = proj[:, 2 * width :]
    keys_t = (keys.astype(F32) * scale).T.astype(BF)
    values_t = values.astype(F32).T.astype(BF)
    out_t, d_q_t = [], []
    d_k = d_v = None
    for pair in range(HEADS // 2):
        hs = (2 * pair, 2 * pair + 1)
        qb = jnp.concatenate([queries * masks[h] for h in hs], axis=0)
        gb = jnp.concatenate([d_out * masks[h] for h in hs], axis=0)
        scores = mt(keys, qb) + bias
        raised = jnp.exp(scores - jnp.max(scores, axis=0, keepdims=True))
        probs = raised * (1.0 / jnp.sum(raised, axis=0, keepdims=True))
        weights = probs.astype(BF)
        grad = mt(values, gb).astype(BF).astype(F32)
        total = jnp.sum(grad * probs, axis=0, keepdims=True)
        d_s = (probs * (grad - total)).astype(BF)
        part_v = mm(weights, gb)
        part_k = mm(d_s, qb)
        d_v = part_v if d_v is None else d_v + part_v
        d_k = part_k if d_k is None else d_k + part_k
        for i, h in enumerate(hs):
            rows = slice(h * size, (h + 1) * size)
            cols = slice(i * 128, (i + 1) * 128)
            out_t.append(mm(values_t[rows], weights[:, cols]))
            d_q_t.append(mm(keys_t[rows], d_s[:, cols]))
    out = jnp.concatenate(out_t, axis=0).T.astype(BF)
    d_q = jnp.concatenate(d_q_t, axis=0).T.astype(BF)
    return out, jnp.concatenate([d_q, d_k.astype(BF), d_v.astype(BF)], axis=1)


def kernel(
    n_arc, n_clu, group,
    deg_ref, feat_ref, cot_ref, wo_ref, wi_ref, wm_ref, order_ref,
    mixed_ref, grad_ref,
    packed, recv, ret, back, res, mix_part, grad_part, flat_row, flat_col,
    send_sem, recv_sem,
):
    rows, width = feat_ref.shape
    cities = rows // K
    per = INNER // n_arc
    slot = cities * per
    edge = cities * INNER
    me = lax.axis_index("arc")
    clu = lax.axis_index("clu")
    nxt, prv = lax.rem(clu + 1, n_clu), lax.rem(clu + n_clu - 1, n_clu)
    mef = me.astype(F32)

    barrier = pltpu.get_barrier_semaphore()
    for s in range(1, n_arc):
        pl.semaphore_signal(
            barrier, inc=1, device_id={"arc": lax.rem(me + s, n_arc)}, device_id_type=MESH
        )
    for other in (nxt, prv):
        pl.semaphore_signal(barrier, inc=1, device_id={"clu": other}, device_id_type=MESH)

    def copy(src, dst, s, leg, target):
        part = pl.ds(s * slot, slot) if s < n_arc else pl.ds(edge, cities * CROSS)
        index = leg * (n_arc + 1) + s
        return pltpu.make_async_remote_copy(
            src_ref=src.at[part],
            dst_ref=dst.at[part],
            send_sem=send_sem.at[index],
            recv_sem=recv_sem.at[index],
            device_id=target,
            device_id_type=MESH,
        )

    out_copies = [copy(packed, recv, n_arc, 0, {"clu": nxt})] + [
        copy(packed, recv, s, 0, {"arc": lax.rem(me + s, n_arc)}) for s in range(1, n_arc)
    ]
    home_copies = [copy(ret, back, n_arc, 1, {"clu": prv})] + [
        copy(ret, back, s, 1, {"arc": lax.rem(me + n_arc - s, n_arc)}) for s in range(1, n_arc)
    ]

    block = group * K
    g_slot = group * per
    g_edge = group * CROSS

    def place(src):
        city = fdiv(src, K)
        arc = src - city * K
        peer = fdiv(arc, per)
        j = arc - peer * per
        s = jnp.where(peer >= mef, peer - mef, peer - mef + n_arc)
        inner = s * g_slot + city * per + j
        return jnp.where(arc < INNER, inner, group * INNER + city * CROSS + (arc - INNER))

    wm = wm_ref[...]
    perm = onehot(place(iota((1, block), 1)), iota((block, block), 0))
    for g in range(cities // group):
        span = pl.ds(g * block, block)
        both = jnp.concatenate([feat_ref[span, :], cot_ref[span, :]], axis=1)
        moved = mm(perm, both).astype(BF)
        d_in = mt(moved[:, width:], wm[width:]).astype(BF)
        moved = jnp.concatenate([moved[:, :width], d_in], axis=1)
        for s in range(n_arc):
            packed[pl.ds(s * slot + g * g_slot, g_slot), :] = moved[s * g_slot : (s + 1) * g_slot]
        packed[pl.ds(edge + g * g_edge, g_edge), :] = moved[group * INNER :]

    pl.semaphore_wait(barrier, n_arc + 1)
    for c in out_copies:
        c.start()
    recv[pl.ds(0, slot), :] = packed[pl.ds(0, slot), :]

    where = order_ref[...].astype(F32)
    city = fdiv(where, INNER)
    arc = where - city * INNER
    peer = fdiv(arc, per)
    j = arc - peer * per
    s = jnp.where(mef >= peer, mef - peer, mef - peer + n_arc)
    where = jnp.where(where < edge, s * slot + city * per + j, where)
    pos = lax.broadcasted_iota(jnp.int32, (1, rows), 1)
    owner = jnp.full((1, rows), -1, jnp.int32)
    start = jnp.zeros((1, rows), jnp.int32)
    offset = jnp.int32(0)
    for t in range(cities):
        begun = pos >= offset
        owner = owner + jnp.where(begun, 1, 0)
        start = jnp.where(begun, offset, start)
        offset = offset + deg_ref[t]
    owner_f = owner.astype(F32)
    local_f = (pos - start).astype(F32)
    line = lax.broadcasted_iota(jnp.int32, (16, rows), 0)
    table = jnp.where(line == 0, owner_f, jnp.where(line == 1, local_f, 0.0)).astype(BF)
    for r in range(rows // 256):
        hits = onehot(where, iota((256, rows), 0) + r * 256)
        found = mt(table, hits)
        flat_row[:, r * 256 : (r + 1) * 256] = jnp.broadcast_to(
            found[0:1] * IN_MAX + found[1:2], (8, 256)
        )
        found = mt(hits, table)
        flat_col[r * 256 : (r + 1) * 256, :] = jnp.broadcast_to(
            found[:, 0:1] * IN_MAX + found[:, 1:2], (256, 128)
        )

    masks = head_masks(width)
    key_city = lax.broadcasted_iota(jnp.int32, (128, 256), 0) >= K
    lane = lax.broadcasted_iota(jnp.int32, (128, 256), 1)
    lane = jnp.where(lane >= 128, lane - 128, lane)
    pair_bias = jnp.where(key_city == (lane >= K), 0.0, -1e30)

    def out_step(c, carry):
        span = pl.ds(pl.multiple_of(c * 128, 128), 128)
        x = feat_ref[span, :]
        u = cot_ref[span, :]
        proj = mm(x, wo_ref[...]).astype(BF)
        d_out = mt(u, wm_ref[:width, :]).astype(BF)
        att, d_proj = attend(proj, d_out, pair_bias, masks)
        mix_part[span, :] = x.astype(F32) + mm(att, wm_ref[:width, :])
        grad_part[span, :] = u.astype(F32) + mt(d_proj, wo_ref[...])
        return carry

    pairs = rows // 128
    lax.fori_loop(0, pairs // 2, out_step, 0)
    for c in out_copies:
        c.wait()

    def in_step(t, carry):
        slots = (lax.broadcasted_iota(jnp.int32, (IN_MAX, rows), 0) + t * IN_MAX).astype(F32)
        pick = onehot(flat_row[0:1, :], slots)
        got = mm(pick, recv[...]).astype(BF)
        proj = mm(got[:, :width], wi_ref[...]).astype(BF)
        live = lax.broadcasted_iota(jnp.int32, (IN_MAX, 256), 0) < deg_ref[t]
        bias = jnp.where(live, 0.0, -1e30)
        att, d_proj = attend(proj, got[:, width:], bias, masks)
        span = pl.ds(pl.multiple_of(t * IN_MAX, IN_MAX), IN_MAX)
        res[span, :width] = att
        res[span, width:] = mt(d_proj, wi_ref[...]).astype(BF)
        return carry

    lax.fori_loop(0, cities, in_step, 0)

    slots = cities * IN_MAX

    def put_back(dst, begin, count):
        pick = onehot(flat_col[begin : begin + count, 0:1], iota((count, slots), 1))
        dst[begin : begin + count, :] = mm(pick, res[...]).astype(BF)

    put_back(ret, edge, cities * CROSS)
    home_copies[0].start()
    for s in range(1, n_arc):
        put_back(ret, s * slot, slot)
        home_copies[s].start()
    put_back(back, 0, slot)
    lax.fori_loop(pairs // 2, pairs, out_step, 0)
    for c in home_copies:
        c.wait()

    perm = onehot(place(iota((block, 1), 0)), iota((block, block), 1))
    for g in range(cities // group):
        moved = [back[pl.ds(s * slot + g * g_slot, g_slot), :] for s in range(n_arc)]
        moved.append(back[pl.ds(edge + g * g_edge, g_edge), :])
        home = mm(perm, jnp.concatenate(moved, axis=0))
        span = pl.ds(g * block, block)
        mixed_ref[span, :] = (
            mix_part[span, :] + mm(home[:, :width].astype(BF), wm[width:])
        ).astype(BF)
        grad_ref[span, :] = (grad_part[span, :] + home[:, width:]).astype(BF)


def body(features, cotangent, w_out_att, w_in_att, w_mix, in_degree, in_order):
    cities, arcs, width = features.shape[2:]
    rows = cities * arcs
    n_arc = lax.axis_size("arc")
    n_clu = lax.axis_size("clu")
    per = INNER // n_arc
    group = next(g for g in (4, 8, 16) if (g * per) % 16 == 0)
    vmem = pl.BlockSpec(memory_space=pltpu.VMEM)
    smem = pl.BlockSpec(memory_space=pltpu.SMEM)
    copies = 2 * (n_arc + 1)
    mixed, grad = pl.pallas_call(
        functools.partial(kernel, n_arc, n_clu, group),
        out_shape=[jax.ShapeDtypeStruct((rows, width), BF)] * 2,
        in_specs=[smem] + [vmem] * 6,
        out_specs=[vmem, vmem],
        scratch_shapes=[
            pltpu.VMEM((rows, 2 * width), BF),
            pltpu.VMEM((rows, 2 * width), BF),
            pltpu.VMEM((rows, 2 * width), BF),
            pltpu.VMEM((rows, 2 * width), BF),
            pltpu.VMEM((cities * IN_MAX, 2 * width), BF),
            pltpu.VMEM((rows, width), F32),
            pltpu.VMEM((rows, width), F32),
            pltpu.VMEM((8, rows), F32),
            pltpu.VMEM((rows, 128), F32),
            pltpu.SemaphoreType.DMA((copies,)),
            pltpu.SemaphoreType.DMA((copies,)),
        ],
        compiler_params=pltpu.CompilerParams(
            collective_id=0, has_side_effects=True, vmem_limit_bytes=48 * 1024 * 1024
        ),
    )(
        in_degree.reshape(cities),
        features.reshape(rows, width),
        cotangent.reshape(rows, width),
        w_out_att,
        w_in_att,
        w_mix,
        in_order.reshape(1, rows),
    )
    return mixed.reshape(features.shape), grad.reshape(features.shape)


def solution(mesh):
    in_specs = (
        P(("grp", "clu"), "arc", None, None, None),
        P(("grp", "clu"), "arc", None, None, None),
        P(),
        P(),
        P(),
        P(("grp", "clu"), "arc", None),
        P(("grp", "clu"), "arc", None),
    )
    out_specs = (
        P(("grp", "clu"), "arc", None, None, None),
        P(("grp", "clu"), "arc", None, None, None),
    )
    return jax.shard_map(body, mesh=mesh, in_specs=in_specs, out_specs=out_specs, check_vma=False)
```

```python
import functools

import jax
import jax.numpy as jnp
from jax import lax
from jax.experimental import pallas as pl
from jax.experimental.pallas import tpu as pltpu
from jax.sharding import PartitionSpec as P

HEADS = 8
K = 64
CROSS = 16
IN_MAX = 128
INNER = K - CROSS
MESH = pl.DeviceIdType.MESH
F32 = jnp.float32
BF = jnp.bfloat16


def mm(a, b):
    return lax.dot_general(a, b, (((1,), (0,)), ((), ())), preferred_element_type=F32)


def mt(a, b):
    return lax.dot_general(a, b, (((1,), (1,)), ((), ())), preferred_element_type=F32)


def iota(shape, dim):
    return lax.broadcasted_iota(jnp.int32, shape, dim).astype(F32)


def fdiv(x, c):
    return jnp.floor((x + 0.5) * (1.0 / c))


def onehot(a, b):
    return jnp.where(a == b, 1.0, 0.0).astype(BF)


def head_masks(width):
    lane = lax.broadcasted_iota(jnp.int32, (16, width), 1)
    size = width // HEADS
    return [
        jnp.where((lane >= h * size) & (lane < (h + 1) * size), 1.0, 0.0).astype(BF)[0:1]
        for h in range(HEADS)
    ]


def attend(proj, d_out, bias, masks):
    width = d_out.shape[1]
    size = width // HEADS
    scale = size ** -0.5
    queries = (proj[:, :width] * scale).astype(BF)
    keys = proj[:, width : 2 * width]
    values = proj[:, 2 * width :]
    keys_t = (keys.astype(F32) * scale).T.astype(BF)
    values_t = values.astype(F32).T.astype(BF)
    qb = jnp.concatenate([queries * m for m in masks], axis=0)
    gb = jnp.concatenate([d_out * m for m in masks], axis=0)
    scores = mt(keys, qb) + jnp.concatenate([bias] * HEADS, axis=1)
    raised = jnp.exp(scores - jnp.max(scores, axis=0, keepdims=True))
    probs = raised * (1.0 / jnp.sum(raised, axis=0, keepdims=True))
    weights = probs.astype(BF)
    grad = mt(values, gb).astype(BF).astype(F32)
    total = jnp.sum(grad * probs, axis=0, keepdims=True)
    d_s = (probs * (grad - total)).astype(BF)
    d_v = mm(weights, gb)
    d_k = mm(d_s, qb)
    out_t, d_q_t = [], []
    for pair in range(HEADS // 2):
        rows = slice(2 * pair * size, 2 * (pair + 1) * size)
        cols = slice(pair * 256, (pair + 1) * 256)
        part = mm(values_t[rows], weights[:, cols])
        out_t += [part[:size, :128], part[size:, 128:]]
        part = mm(keys_t[rows], d_s[:, cols])
        d_q_t += [part[:size, :128], part[size:, 128:]]
    out = jnp.concatenate(out_t, axis=0).T.astype(BF)
    d_q = jnp.concatenate(d_q_t, axis=0).T.astype(BF)
    return out, jnp.concatenate([d_q, d_k.astype(BF), d_v.astype(BF)], axis=1)


def kernel(
    n_arc, n_clu, group,
    deg_ref, feat_hbm, cot_hbm, wo_hbm, wi_hbm, wm_hbm, order_ref,
    mixed_ref, grad_ref,
    feat_ref, cot_ref, wo_ref, wi_ref, wm_ref,
    packed, recv, ret, back, res, mix_part, grad_part, flat_row, flat_col,
    send_sem, recv_sem, load_sem,
):
    loads = [
        pltpu.make_async_copy(src, dst, load_sem.at[i])
        for i, (src, dst) in enumerate(
            [
                (feat_hbm, feat_ref),
                (cot_hbm, cot_ref),
                (wm_hbm, wm_ref),
                (wo_hbm, wo_ref),
                (wi_hbm, wi_ref),
            ]
        )
    ]
    for c in loads:
        c.start()
    rows, width = feat_ref.shape
    cities = rows // K
    per = INNER // n_arc
    slot = cities * per
    edge = cities * INNER
    me = lax.axis_index("arc")
    clu = lax.axis_index("clu")
    nxt, prv = lax.rem(clu + 1, n_clu), lax.rem(clu + n_clu - 1, n_clu)
    mef = me.astype(F32)

    barrier = pltpu.get_barrier_semaphore()
    for s in range(1, n_arc):
        pl.semaphore_signal(
            barrier, inc=1, device_id={"arc": lax.rem(me + s, n_arc)}, device_id_type=MESH
        )
    for other in (nxt, prv):
        pl.semaphore_signal(barrier, inc=1, device_id={"clu": other}, device_id_type=MESH)

    def copy(src, dst, s, leg, target):
        part = pl.ds(s * slot, slot) if s < n_arc else pl.ds(edge, cities * CROSS)
        index = leg * (n_arc + 1) + s
        return pltpu.make_async_remote_copy(
            src_ref=src.at[part],
            dst_ref=dst.at[part],
            send_sem=send_sem.at[index],
            recv_sem=recv_sem.at[index],
            device_id=target,
            device_id_type=MESH,
        )

    out_copies = [copy(packed, recv, n_arc, 0, {"clu": nxt})] + [
        copy(packed, recv, s, 0, {"arc": lax.rem(me + s, n_arc)}) for s in range(1, n_arc)
    ]
    home_copies = [copy(ret, back, n_arc, 1, {"clu": prv})] + [
        copy(ret, back, s, 1, {"arc": lax.rem(me + n_arc - s, n_arc)}) for s in range(1, n_arc)
    ]

    block = group * K
    g_slot = group * per
    g_edge = group * CROSS

    def place(src):
        city = fdiv(src, K)
        arc = src - city * K
        peer = fdiv(arc, per)
        j = arc - peer * per
        s = jnp.where(peer >= mef, peer - mef, peer - mef + n_arc)
        inner = s * g_slot + city * per + j
        return jnp.where(arc < INNER, inner, group * INNER + city * CROSS + (arc - INNER))

    perm = onehot(place(iota((1, block), 1)), iota((block, block), 0))
    for c in loads:
        c.wait()
    wm = wm_ref[...]
    for g in range(cities // group):
        span = pl.ds(g * block, block)
        both = jnp.concatenate([feat_ref[span, :], cot_ref[span, :]], axis=1)
        moved = mm(perm, both).astype(BF)
        d_in = mt(moved[:, width:], wm[width:]).astype(BF)
        moved = jnp.concatenate([moved[:, :width], d_in], axis=1)
        for s in range(n_arc):
            packed[pl.ds(s * slot + g * g_slot, g_slot), :] = moved[s * g_slot : (s + 1) * g_slot]
        packed[pl.ds(edge + g * g_edge, g_edge), :] = moved[group * INNER :]

    pl.semaphore_wait(barrier, n_arc + 1)
    for c in out_copies:
        c.start()
    recv[pl.ds(0, slot), :] = packed[pl.ds(0, slot), :]

    where = order_ref[...].astype(F32)
    city = fdiv(where, INNER)
    arc = where - city * INNER
    peer = fdiv(arc, per)
    j = arc - peer * per
    s = jnp.where(mef >= peer, mef - peer, mef - peer + n_arc)
    where = jnp.where(where < edge, s * slot + city * per + j, where)
    pos = lax.broadcasted_iota(jnp.int32, (1, rows), 1)
    owner = jnp.full((1, rows), -1, jnp.int32)
    start = jnp.zeros((1, rows), jnp.int32)
    offset = jnp.int32(0)
    for t in range(cities):
        begun = pos >= offset
        owner = owner + jnp.where(begun, 1, 0)
        start = jnp.where(begun, offset, start)
        offset = offset + deg_ref[t]
    owner_f = owner.astype(F32)
    local_f = (pos - start).astype(F32)
    line = lax.broadcasted_iota(jnp.int32, (16, rows), 0)
    table = jnp.where(line == 0, owner_f, jnp.where(line == 1, local_f, 0.0)).astype(BF)
    for r in range(rows // 256):
        hits = onehot(where, iota((256, rows), 0) + r * 256)
        found = mt(table, hits)
        flat_row[:, r * 256 : (r + 1) * 256] = jnp.broadcast_to(
            found[0:1] * IN_MAX + found[1:2], (8, 256)
        )
        found = mt(hits, table)
        flat_col[r * 256 : (r + 1) * 256, :] = jnp.broadcast_to(
            found[:, 0:1] * IN_MAX + found[:, 1:2], (256, 128)
        )

    masks = head_masks(width)
    key_row = lax.broadcasted_iota(jnp.int32, (128, 128), 0)
    lane = lax.broadcasted_iota(jnp.int32, (128, 128), 1)
    split = (key_row - K + 0.5).astype(F32) * (lane - K + 0.5).astype(F32)
    pair_bias = jnp.where(split > 0, 0.0, -1e30)

    def out_step(c, carry):
        span = pl.ds(pl.multiple_of(c * 128, 128), 128)
        x = feat_ref[span, :]
        u = cot_ref[span, :]
        proj = mm(x, wo_ref[...]).astype(BF)
        d_out = mt(u, wm_ref[:width, :]).astype(BF)
        att, d_proj = attend(proj, d_out, pair_bias, masks)
        mix_part[span, :] = x.astype(F32) + mm(att, wm_ref[:width, :])
        grad_part[span, :] = u.astype(F32) + mt(d_proj, wo_ref[...])
        return carry

    pairs = rows // 128
    lax.fori_loop(0, pairs // 2, out_step, 0, unroll=2)
    for c in out_copies:
        c.wait()

    def in_step(t, carry):
        slots = (lax.broadcasted_iota(jnp.int32, (IN_MAX, rows), 0) + t * IN_MAX).astype(F32)
        pick = onehot(flat_row[0:1, :], slots)
        got = mm(pick, recv[...]).astype(BF)
        proj = mm(got[:, :width], wi_ref[...]).astype(BF)
        live = lax.broadcasted_iota(jnp.int32, (IN_MAX, IN_MAX), 0) < deg_ref[t]
        bias = jnp.where(live, 0.0, -1e30)
        att, d_proj = attend(proj, got[:, width:], bias, masks)
        span = pl.ds(pl.multiple_of(t * IN_MAX, IN_MAX), IN_MAX)
        res[span, :width] = att
        res[span, width:] = mt(d_proj, wi_ref[...]).astype(BF)
        return carry

    lax.fori_loop(0, cities, in_step, 0, unroll=2)

    slots = cities * IN_MAX

    def put_back(dst, begin, count):
        pick = onehot(flat_col[begin : begin + count, 0:1], iota((count, slots), 1))
        dst[begin : begin + count, :] = mm(pick, res[...]).astype(BF)

    put_back(ret, edge, cities * CROSS)
    home_copies[0].start()
    for s in range(1, n_arc):
        put_back(ret, s * slot, slot)
        home_copies[s].start()
    put_back(back, 0, slot)
    lax.fori_loop(pairs // 2, pairs, out_step, 0, unroll=2)
    for c in home_copies:
        c.wait()

    perm = onehot(place(iota((block, 1), 0)), iota((block, block), 1))
    for g in range(cities // group):
        moved = [back[pl.ds(s * slot + g * g_slot, g_slot), :] for s in range(n_arc)]
        moved.append(back[pl.ds(edge + g * g_edge, g_edge), :])
        home = mm(perm, jnp.concatenate(moved, axis=0))
        span = pl.ds(g * block, block)
        mixed_ref[span, :] = (
            mix_part[span, :] + mm(home[:, :width].astype(BF), wm[width:])
        ).astype(BF)
        grad_ref[span, :] = (grad_part[span, :] + home[:, width:]).astype(BF)


def body(features, cotangent, w_out_att, w_in_att, w_mix, in_degree, in_order):
    cities, arcs, width = features.shape[2:]
    rows = cities * arcs
    n_arc = lax.axis_size("arc")
    n_clu = lax.axis_size("clu")
    per = INNER // n_arc
    group = next(g for g in (4, 8, 16) if (g * per) % 16 == 0)
    vmem = pl.BlockSpec(memory_space=pltpu.VMEM)
    smem = pl.BlockSpec(memory_space=pltpu.SMEM)
    copies = 2 * (n_arc + 1)
    mixed, grad = pl.pallas_call(
        functools.partial(kernel, n_arc, n_clu, group),
        out_shape=[jax.ShapeDtypeStruct((rows, width), BF)] * 2,
        in_specs=[smem] + [pl.BlockSpec(memory_space=pltpu.HBM)] * 5 + [vmem],
        out_specs=[vmem, vmem],
        scratch_shapes=[
            pltpu.VMEM((rows, width), BF),
            pltpu.VMEM((rows, width), BF),
            pltpu.VMEM(w_out_att.shape, BF),
            pltpu.VMEM(w_in_att.shape, BF),
            pltpu.VMEM(w_mix.shape, BF),
            pltpu.VMEM((rows, 2 * width), BF),
            pltpu.VMEM((rows, 2 * width), BF),
            pltpu.VMEM((rows, 2 * width), BF),
            pltpu.VMEM((rows, 2 * width), BF),
            pltpu.VMEM((cities * IN_MAX, 2 * width), BF),
            pltpu.VMEM((rows, width), F32),
            pltpu.VMEM((rows, width), F32),
            pltpu.VMEM((8, rows), F32),
            pltpu.VMEM((rows, 128), F32),
            pltpu.SemaphoreType.DMA((copies,)),
            pltpu.SemaphoreType.DMA((copies,)),
            pltpu.SemaphoreType.DMA((5,)),
        ],
        compiler_params=pltpu.CompilerParams(
            collective_id=0, has_side_effects=True, vmem_limit_bytes=48 * 1024 * 1024
        ),
    )(
        in_degree.reshape(cities),
        features.reshape(rows, width),
        cotangent.reshape(rows, width),
        w_out_att,
        w_in_att,
        w_mix,
        in_order.reshape(1, rows),
    )
    return mixed.reshape(features.shape), grad.reshape(features.shape)


def solution(mesh):
    in_specs = (
        P(("grp", "clu"), "arc", None, None, None),
        P(("grp", "clu"), "arc", None, None, None),
        P(),
        P(),
        P(),
        P(("grp", "clu"), "arc", None),
        P(("grp", "clu"), "arc", None),
    )
    out_specs = (
        P(("grp", "clu"), "arc", None, None, None),
        P(("grp", "clu"), "arc", None, None, None),
    )
    return jax.shard_map(body, mesh=mesh, in_specs=in_specs, out_specs=out_specs, check_vma=False)
```

```python
import functools

import jax
import jax.numpy as jnp
from jax import lax
from jax.experimental import pallas as pl
from jax.experimental.pallas import tpu as pltpu
from jax.sharding import PartitionSpec as P

HEADS = 8
K = 64
CROSS = 16
IN_MAX = 128
INNER = K - CROSS
MESH = pl.DeviceIdType.MESH
F32 = jnp.float32
BF = jnp.bfloat16


def mm(a, b):
    return lax.dot_general(a, b, (((1,), (0,)), ((), ())), preferred_element_type=F32)


def mt(a, b):
    return lax.dot_general(a, b, (((1,), (1,)), ((), ())), preferred_element_type=F32)


def iota(shape, dim):
    return lax.broadcasted_iota(jnp.int32, shape, dim).astype(F32)


def fdiv(x, c):
    return jnp.floor((x + 0.5) * (1.0 / c))


def onehot(a, b):
    return jnp.where(a == b, 1.0, 0.0).astype(BF)


def head_masks(width):
    lane = lax.broadcasted_iota(jnp.int32, (16, width), 1)
    size = width // HEADS
    return [
        jnp.where((lane >= h * size) & (lane < (h + 1) * size), 1.0, 0.0).astype(BF)[0:1]
        for h in range(HEADS)
    ]


def attend(proj, d_out, bias, masks):
    width = d_out.shape[1]
    size = width // HEADS
    scale = size ** -0.5
    queries = (proj[:, :width] * scale).astype(BF)
    keys = proj[:, width : 2 * width]
    values = proj[:, 2 * width :]
    keys_t = (keys.astype(F32) * scale).T.astype(BF)
    values_t = values.astype(F32).T.astype(BF)
    qb = jnp.concatenate([queries * m for m in masks], axis=0)
    gb = jnp.concatenate([d_out * m for m in masks], axis=0)
    scores = mt(keys, qb) + jnp.concatenate([bias] * HEADS, axis=1)
    raised = jnp.exp(scores - jnp.max(scores, axis=0, keepdims=True))
    probs = raised * (1.0 / jnp.sum(raised, axis=0, keepdims=True))
    weights = probs.astype(BF)
    grad = mt(values, gb).astype(BF).astype(F32)
    total = jnp.sum(grad * probs, axis=0, keepdims=True)
    d_s = (probs * (grad - total)).astype(BF)
    d_v = mm(weights, gb)
    d_k = mm(d_s, qb)
    out_t, d_q_t = [], []
    for pair in range(HEADS // 2):
        rows = slice(2 * pair * size, 2 * (pair + 1) * size)
        cols = slice(pair * 256, (pair + 1) * 256)
        part = mm(values_t[rows], weights[:, cols])
        out_t += [part[:size, :128], part[size:, 128:]]
        part = mm(keys_t[rows], d_s[:, cols])
        d_q_t += [part[:size, :128], part[size:, 128:]]
    out = jnp.concatenate(out_t, axis=0).T.astype(BF)
    d_q = jnp.concatenate(d_q_t, axis=0).T.astype(BF)
    return out, jnp.concatenate([d_q, d_k.astype(BF), d_v.astype(BF)], axis=1)


def kernel(
    n_arc, n_clu, group,
    deg_ref, feat_hbm, cot_hbm, wo_hbm, wi_hbm, wm_hbm, order_ref,
    mixed_ref, grad_ref,
    feat_ref, cot_ref, wo_ref, wi_ref, wm_ref, proj_in, d_got,
    packed, recv, ret, back, res, mix_part, grad_part, flat_row, flat_col,
    send_sem, recv_sem, load_sem,
):
    loads = [
        pltpu.make_async_copy(src, dst, load_sem.at[i])
        for i, (src, dst) in enumerate(
            [
                (feat_hbm, feat_ref),
                (cot_hbm, cot_ref),
                (wm_hbm, wm_ref),
                (wo_hbm, wo_ref),
                (wi_hbm, wi_ref),
            ]
        )
    ]
    for c in loads:
        c.start()
    rows, width = feat_ref.shape
    cities = rows // K
    per = INNER // n_arc
    slot = cities * per
    edge = cities * INNER
    me = lax.axis_index("arc")
    clu = lax.axis_index("clu")
    nxt, prv = lax.rem(clu + 1, n_clu), lax.rem(clu + n_clu - 1, n_clu)
    mef = me.astype(F32)

    barrier = pltpu.get_barrier_semaphore()
    for s in range(1, n_arc):
        pl.semaphore_signal(
            barrier, inc=1, device_id={"arc": lax.rem(me + s, n_arc)}, device_id_type=MESH
        )
    for other in (nxt, prv):
        pl.semaphore_signal(barrier, inc=1, device_id={"clu": other}, device_id_type=MESH)

    def copy(src, dst, s, leg, target):
        part = pl.ds(s * slot, slot) if s < n_arc else pl.ds(edge, cities * CROSS)
        index = leg * (n_arc + 1) + s
        return pltpu.make_async_remote_copy(
            src_ref=src.at[part],
            dst_ref=dst.at[part],
            send_sem=send_sem.at[index],
            recv_sem=recv_sem.at[index],
            device_id=target,
            device_id_type=MESH,
        )

    out_copies = [copy(packed, recv, n_arc, 0, {"clu": nxt})] + [
        copy(packed, recv, s, 0, {"arc": lax.rem(me + s, n_arc)}) for s in range(1, n_arc)
    ]
    home_copies = [copy(ret, back, n_arc, 1, {"clu": prv})] + [
        copy(ret, back, s, 1, {"arc": lax.rem(me + n_arc - s, n_arc)}) for s in range(1, n_arc)
    ]

    block = group * K
    g_slot = group * per
    g_edge = group * CROSS

    def place(src):
        city = fdiv(src, K)
        arc = src - city * K
        peer = fdiv(arc, per)
        j = arc - peer * per
        s = jnp.where(peer >= mef, peer - mef, peer - mef + n_arc)
        inner = s * g_slot + city * per + j
        return jnp.where(arc < INNER, inner, group * INNER + city * CROSS + (arc - INNER))

    perm = onehot(place(iota((1, block), 1)), iota((block, block), 0))
    for c in loads:
        c.wait()
    wm = wm_ref[...]
    for g in range(cities // group):
        span = pl.ds(g * block, block)
        both = jnp.concatenate([feat_ref[span, :], cot_ref[span, :]], axis=1)
        moved = mm(perm, both).astype(BF)
        d_in = mt(moved[:, width:], wm[width:]).astype(BF)
        moved = jnp.concatenate([moved[:, :width], d_in], axis=1)
        for s in range(n_arc):
            packed[pl.ds(s * slot + g * g_slot, g_slot), :] = moved[s * g_slot : (s + 1) * g_slot]
        packed[pl.ds(edge + g * g_edge, g_edge), :] = moved[group * INNER :]

    pl.semaphore_wait(barrier, n_arc + 1)
    for c in out_copies:
        c.start()
    recv[pl.ds(0, slot), :] = packed[pl.ds(0, slot), :]

    where = order_ref[...].astype(F32)
    city = fdiv(where, INNER)
    arc = where - city * INNER
    peer = fdiv(arc, per)
    j = arc - peer * per
    s = jnp.where(mef >= peer, mef - peer, mef - peer + n_arc)
    where = jnp.where(where < edge, s * slot + city * per + j, where)
    pos = lax.broadcasted_iota(jnp.int32, (1, rows), 1)
    owner = jnp.full((1, rows), -1, jnp.int32)
    start = jnp.zeros((1, rows), jnp.int32)
    offset = jnp.int32(0)
    for t in range(cities):
        begun = pos >= offset
        owner = owner + jnp.where(begun, 1, 0)
        start = jnp.where(begun, offset, start)
        offset = offset + deg_ref[t]
    owner_f = owner.astype(F32)
    local_f = (pos - start).astype(F32)
    line = lax.broadcasted_iota(jnp.int32, (16, rows), 0)
    table = jnp.where(line == 0, owner_f, jnp.where(line == 1, local_f, 0.0)).astype(BF)
    for r in range(rows // 256):
        hits = onehot(where, iota((256, rows), 0) + r * 256)
        found = mt(table, hits)
        flat_row[:, r * 256 : (r + 1) * 256] = jnp.broadcast_to(
            found[0:1] * IN_MAX + found[1:2], (8, 256)
        )
        found = mt(hits, table)
        flat_col[r * 256 : (r + 1) * 256, :] = jnp.broadcast_to(
            found[:, 0:1] * IN_MAX + found[:, 1:2], (256, 128)
        )

    masks = head_masks(width)
    key_row = lax.broadcasted_iota(jnp.int32, (128, 128), 0)
    lane = lax.broadcasted_iota(jnp.int32, (128, 128), 1)
    split = (key_row - K + 0.5).astype(F32) * (lane - K + 0.5).astype(F32)
    pair_bias = jnp.where(split > 0, 0.0, -1e30)

    def out_step(c, carry):
        span = pl.ds(pl.multiple_of(c * 128, 128), 128)
        x = feat_ref[span, :]
        u = cot_ref[span, :]
        proj = mm(x, wo_ref[...]).astype(BF)
        d_out = mt(u, wm_ref[:width, :]).astype(BF)
        att, d_proj = attend(proj, d_out, pair_bias, masks)
        mix_part[span, :] = x.astype(F32) + mm(att, wm_ref[:width, :])
        grad_part[span, :] = u.astype(F32) + mt(d_proj, wo_ref[...])
        return carry

    pairs = rows // 128
    lax.fori_loop(0, pairs // 2, out_step, 0, unroll=2)
    for c in out_copies:
        c.wait()

    def gather_step(b, carry):
        slots = (lax.broadcasted_iota(jnp.int32, (512, rows), 0) + b * 512).astype(F32)
        pick = onehot(flat_row[0:1, :], slots)
        got = mm(pick, recv[...]).astype(BF)
        span = pl.ds(pl.multiple_of(b * 512, 512), 512)
        proj_in[span, :] = mm(got[:, :width], wi_ref[...]).astype(BF)
        d_got[span, :] = got[:, width:]
        return carry

    def in_step(t, carry):
        live = lax.broadcasted_iota(jnp.int32, (IN_MAX, IN_MAX), 0) < deg_ref[t]
        bias = jnp.where(live, 0.0, -1e30)
        span = pl.ds(pl.multiple_of(t * IN_MAX, IN_MAX), IN_MAX)
        att, d_proj = attend(proj_in[span, :], d_got[span, :], bias, masks)
        res[span, :width] = att
        proj_in[span, :] = d_proj
        return carry

    def pull_step(b, carry):
        span = pl.ds(pl.multiple_of(b * 512, 512), 512)
        res[span, width:] = mt(proj_in[span, :], wi_ref[...]).astype(BF)
        return carry

    lax.fori_loop(0, cities * IN_MAX // 512, gather_step, 0)
    lax.fori_loop(0, cities, in_step, 0, unroll=2)
    lax.fori_loop(0, cities * IN_MAX // 512, pull_step, 0)

    slots = cities * IN_MAX

    def put_back(dst, begin, count):
        pick = onehot(flat_col[begin : begin + count, 0:1], iota((count, slots), 1))
        dst[begin : begin + count, :] = mm(pick, res[...]).astype(BF)

    put_back(ret, edge, cities * CROSS)
    home_copies[0].start()
    for s in range(1, n_arc):
        put_back(ret, s * slot, slot)
        home_copies[s].start()
    put_back(back, 0, slot)
    lax.fori_loop(pairs // 2, pairs, out_step, 0, unroll=2)
    for c in home_copies:
        c.wait()

    perm = onehot(place(iota((block, 1), 0)), iota((block, block), 1))
    for g in range(cities // group):
        moved = [back[pl.ds(s * slot + g * g_slot, g_slot), :] for s in range(n_arc)]
        moved.append(back[pl.ds(edge + g * g_edge, g_edge), :])
        home = mm(perm, jnp.concatenate(moved, axis=0))
        span = pl.ds(g * block, block)
        mixed_ref[span, :] = (
            mix_part[span, :] + mm(home[:, :width].astype(BF), wm[width:])
        ).astype(BF)
        grad_ref[span, :] = (grad_part[span, :] + home[:, width:]).astype(BF)


def body(features, cotangent, w_out_att, w_in_att, w_mix, in_degree, in_order):
    cities, arcs, width = features.shape[2:]
    rows = cities * arcs
    n_arc = lax.axis_size("arc")
    n_clu = lax.axis_size("clu")
    per = INNER // n_arc
    group = next(g for g in (4, 8, 16) if (g * per) % 16 == 0)
    vmem = pl.BlockSpec(memory_space=pltpu.VMEM)
    smem = pl.BlockSpec(memory_space=pltpu.SMEM)
    copies = 2 * (n_arc + 1)
    mixed, grad = pl.pallas_call(
        functools.partial(kernel, n_arc, n_clu, group),
        out_shape=[jax.ShapeDtypeStruct((rows, width), BF)] * 2,
        in_specs=[smem] + [pl.BlockSpec(memory_space=pltpu.HBM)] * 5 + [vmem],
        out_specs=[vmem, vmem],
        scratch_shapes=[
            pltpu.VMEM((rows, width), BF),
            pltpu.VMEM((rows, width), BF),
            pltpu.VMEM(w_out_att.shape, BF),
            pltpu.VMEM(w_in_att.shape, BF),
            pltpu.VMEM(w_mix.shape, BF),
            pltpu.VMEM((cities * IN_MAX, 3 * width), BF),
            pltpu.VMEM((cities * IN_MAX, width), BF),
            pltpu.VMEM((rows, 2 * width), BF),
            pltpu.VMEM((rows, 2 * width), BF),
            pltpu.VMEM((rows, 2 * width), BF),
            pltpu.VMEM((rows, 2 * width), BF),
            pltpu.VMEM((cities * IN_MAX, 2 * width), BF),
            pltpu.VMEM((rows, width), F32),
            pltpu.VMEM((rows, width), F32),
            pltpu.VMEM((8, rows), F32),
            pltpu.VMEM((rows, 128), F32),
            pltpu.SemaphoreType.DMA((copies,)),
            pltpu.SemaphoreType.DMA((copies,)),
            pltpu.SemaphoreType.DMA((5,)),
        ],
        compiler_params=pltpu.CompilerParams(
            collective_id=0, has_side_effects=True, vmem_limit_bytes=63*1024*1024
        ),
    )(
        in_degree.reshape(cities),
        features.reshape(rows, width),
        cotangent.reshape(rows, width),
        w_out_att,
        w_in_att,
        w_mix,
        in_order.reshape(1, rows),
    )
    return mixed.reshape(features.shape), grad.reshape(features.shape)


def solution(mesh):
    in_specs = (
        P(("grp", "clu"), "arc", None, None, None),
        P(("grp", "clu"), "arc", None, None, None),
        P(),
        P(),
        P(),
        P(("grp", "clu"), "arc", None),
        P(("grp", "clu"), "arc", None),
    )
    out_specs = (
        P(("grp", "clu"), "arc", None, None, None),
        P(("grp", "clu"), "arc", None, None, None),
    )
    return jax.shard_map(body, mesh=mesh, in_specs=in_specs, out_specs=out_specs, check_vma=False)
```

```python
import functools

import jax
import jax.numpy as jnp
from jax import lax
from jax.experimental import pallas as pl
from jax.experimental.pallas import tpu as pltpu
from jax.sharding import PartitionSpec as P

HEADS = 8
K = 64
CROSS = 16
IN_MAX = 128
INNER = K - CROSS
MESH = pl.DeviceIdType.MESH
F32 = jnp.float32
BF = jnp.bfloat16


def mm(a, b):
    return lax.dot_general(a, b, (((1,), (0,)), ((), ())), preferred_element_type=F32)


def mt(a, b):
    return lax.dot_general(a, b, (((1,), (1,)), ((), ())), preferred_element_type=F32)


def iota(shape, dim):
    return lax.broadcasted_iota(jnp.int32, shape, dim).astype(F32)


def fdiv(x, c):
    return jnp.floor((x + 0.5) * (1.0 / c))


def onehot(a, b):
    return jnp.where(a == b, 1.0, 0.0).astype(BF)


def head_masks(width):
    lane = lax.broadcasted_iota(jnp.int32, (16, width), 1)
    size = width // HEADS
    return [
        jnp.where((lane >= h * size) & (lane < (h + 1) * size), 1.0, 0.0).astype(BF)[0:1]
        for h in range(HEADS)
    ]


def attend(proj, d_out, bias, masks):
    width = d_out.shape[1]
    size = width // HEADS
    scale = size ** -0.5
    queries = (proj[:, :width] * scale).astype(BF)
    keys = proj[:, width : 2 * width]
    values = proj[:, 2 * width :]
    keys_t = (keys.astype(F32) * scale).T.astype(BF)
    values_t = values.astype(F32).T.astype(BF)
    qb = jnp.concatenate([queries * m for m in masks], axis=0)
    gb = jnp.concatenate([d_out * m for m in masks], axis=0)
    scores = mt(keys, qb) + jnp.concatenate([bias] * HEADS, axis=1)
    raised = jnp.exp(scores - jnp.max(scores, axis=0, keepdims=True))
    probs = raised * (1.0 / jnp.sum(raised, axis=0, keepdims=True))
    weights = probs.astype(BF)
    grad = mt(values, gb).astype(BF).astype(F32)
    total = jnp.sum(grad * probs, axis=0, keepdims=True)
    d_s = (probs * (grad - total)).astype(BF)
    d_v = mm(weights, gb)
    d_k = mm(d_s, qb)
    out_t, d_q_t = [], []
    for pair in range(HEADS // 2):
        rows = slice(2 * pair * size, 2 * (pair + 1) * size)
        cols = slice(pair * 256, (pair + 1) * 256)
        part = mm(values_t[rows], weights[:, cols])
        out_t += [part[:size, :128], part[size:, 128:]]
        part = mm(keys_t[rows], d_s[:, cols])
        d_q_t += [part[:size, :128], part[size:, 128:]]
    out = jnp.concatenate(out_t, axis=0).T.astype(BF)
    d_q = jnp.concatenate(d_q_t, axis=0).T.astype(BF)
    return out, jnp.concatenate([d_q, d_k.astype(BF), d_v.astype(BF)], axis=1)


def kernel(
    n_arc, n_clu, group,
    deg_ref, feat_hbm, cot_hbm, wo_hbm, wi_hbm, wm_hbm, order_ref,
    mixed_ref, grad_ref,
    feat_ref, cot_ref, wo_ref, wi_ref, wm_ref, proj_in, d_got,
    packed, recv, ret, back, res, mix_part, grad_part, flat_row, flat_col,
    send_sem, recv_sem, load_sem,
):
    loads = [
        pltpu.make_async_copy(src, dst, load_sem.at[i])
        for i, (src, dst) in enumerate(
            [
                (feat_hbm, feat_ref),
                (cot_hbm, cot_ref),
                (wm_hbm, wm_ref),
                (wo_hbm, wo_ref),
                (wi_hbm, wi_ref),
            ]
        )
    ]
    for c in loads:
        c.start()
    rows, width = feat_ref.shape
    cities = rows // K
    per = INNER // n_arc
    slot = cities * per
    edge = cities * INNER
    me = lax.axis_index("arc")
    clu = lax.axis_index("clu")
    nxt, prv = lax.rem(clu + 1, n_clu), lax.rem(clu + n_clu - 1, n_clu)
    mef = me.astype(F32)

    barrier = pltpu.get_barrier_semaphore()
    for s in range(1, n_arc):
        pl.semaphore_signal(
            barrier, inc=1, device_id={"arc": lax.rem(me + s, n_arc)}, device_id_type=MESH
        )
    for other in (nxt, prv):
        pl.semaphore_signal(barrier, inc=1, device_id={"clu": other}, device_id_type=MESH)

    def copy(src, dst, s, leg, target):
        part = pl.ds(s * slot, slot) if s < n_arc else pl.ds(edge, cities * CROSS)
        index = leg * (n_arc + 1) + s
        return pltpu.make_async_remote_copy(
            src_ref=src.at[part],
            dst_ref=dst.at[part],
            send_sem=send_sem.at[index],
            recv_sem=recv_sem.at[index],
            device_id=target,
            device_id_type=MESH,
        )

    far = sorted(range(1, n_arc), key=lambda s: abs(2 * s - n_arc))
    out_copies = [
        copy(packed, recv, s, 0, {"arc": lax.rem(me + s, n_arc)}) for s in far
    ] + [copy(packed, recv, n_arc, 0, {"clu": nxt})]
    home_copies = [copy(ret, back, n_arc, 1, {"clu": prv})] + [
        copy(ret, back, s, 1, {"arc": lax.rem(me + n_arc - s, n_arc)}) for s in range(1, n_arc)
    ]

    block = group * K
    g_slot = group * per
    g_edge = group * CROSS

    def place(src):
        city = fdiv(src, K)
        arc = src - city * K
        peer = fdiv(arc, per)
        j = arc - peer * per
        s = jnp.where(peer >= mef, peer - mef, peer - mef + n_arc)
        inner = s * g_slot + city * per + j
        return jnp.where(arc < INNER, inner, group * INNER + city * CROSS + (arc - INNER))

    perm = onehot(place(iota((1, block), 1)), iota((block, block), 0))
    for c in loads:
        c.wait()
    wm = wm_ref[...]
    for g in range(cities // group):
        span = pl.ds(g * block, block)
        both = jnp.concatenate([feat_ref[span, :], cot_ref[span, :]], axis=1)
        moved = mm(perm, both).astype(BF)
        d_in = mt(moved[:, width:], wm[width:]).astype(BF)
        moved = jnp.concatenate([moved[:, :width], d_in], axis=1)
        for s in range(n_arc):
            packed[pl.ds(s * slot + g * g_slot, g_slot), :] = moved[s * g_slot : (s + 1) * g_slot]
        packed[pl.ds(edge + g * g_edge, g_edge), :] = moved[group * INNER :]

    pl.semaphore_wait(barrier, n_arc + 1)
    for c in out_copies:
        c.start()
    recv[pl.ds(0, slot), :] = packed[pl.ds(0, slot), :]

    where = order_ref[...].astype(F32)
    city = fdiv(where, INNER)
    arc = where - city * INNER
    peer = fdiv(arc, per)
    j = arc - peer * per
    s = jnp.where(mef >= peer, mef - peer, mef - peer + n_arc)
    where = jnp.where(where < edge, s * slot + city * per + j, where)
    pos = lax.broadcasted_iota(jnp.int32, (1, rows), 1)
    owner = jnp.full((1, rows), -1, jnp.int32)
    start = jnp.zeros((1, rows), jnp.int32)
    offset = jnp.int32(0)
    for t in range(cities):
        begun = pos >= offset
        owner = owner + jnp.where(begun, 1, 0)
        start = jnp.where(begun, offset, start)
        offset = offset + deg_ref[t]
    owner_f = owner.astype(F32)
    local_f = (pos - start).astype(F32)
    line = lax.broadcasted_iota(jnp.int32, (16, rows), 0)
    table = jnp.where(line == 0, owner_f, jnp.where(line == 1, local_f, 0.0)).astype(BF)
    for r in range(rows // 256):
        hits = onehot(where, iota((256, rows), 0) + r * 256)
        found = mt(table, hits)
        flat_row[:, r * 256 : (r + 1) * 256] = jnp.broadcast_to(
            found[0:1] * IN_MAX + found[1:2], (8, 256)
        )
        found = mt(hits, table)
        flat_col[r * 256 : (r + 1) * 256, :] = jnp.broadcast_to(
            found[:, 0:1] * IN_MAX + found[:, 1:2], (256, 128)
        )

    masks = head_masks(width)
    key_row = lax.broadcasted_iota(jnp.int32, (128, 128), 0)
    lane = lax.broadcasted_iota(jnp.int32, (128, 128), 1)
    split = (key_row - K + 0.5).astype(F32) * (lane - K + 0.5).astype(F32)
    pair_bias = jnp.where(split > 0, 0.0, -1e30)

    def out_step(c, carry):
        span = pl.ds(pl.multiple_of(c * 128, 128), 128)
        x = feat_ref[span, :]
        u = cot_ref[span, :]
        proj = mm(x, wo_ref[...]).astype(BF)
        d_out = mt(u, wm_ref[:width, :]).astype(BF)
        att, d_proj = attend(proj, d_out, pair_bias, masks)
        mix_part[span, :] = x.astype(F32) + mm(att, wm_ref[:width, :])
        grad_part[span, :] = u.astype(F32) + mt(d_proj, wo_ref[...])
        return carry

    pairs = rows // 128
    lax.fori_loop(0, pairs // 2, out_step, 0, unroll=2)
    for c in out_copies:
        c.wait()

    def gather_step(b, carry):
        slots = (lax.broadcasted_iota(jnp.int32, (512, rows), 0) + b * 512).astype(F32)
        pick = onehot(flat_row[0:1, :], slots)
        got = mm(pick, recv[...]).astype(BF)
        span = pl.ds(pl.multiple_of(b * 512, 512), 512)
        proj_in[span, :] = mm(got[:, :width], wi_ref[...]).astype(BF)
        d_got[span, :] = got[:, width:]
        return carry

    def in_step(t, carry):
        live = lax.broadcasted_iota(jnp.int32, (IN_MAX, IN_MAX), 0) < deg_ref[t]
        bias = jnp.where(live, 0.0, -1e30)
        span = pl.ds(pl.multiple_of(t * IN_MAX, IN_MAX), IN_MAX)
        att, d_proj = attend(proj_in[span, :], d_got[span, :], bias, masks)
        res[span, :width] = att
        proj_in[span, :] = d_proj
        return carry

    def pull_step(b, carry):
        span = pl.ds(pl.multiple_of(b * 512, 512), 512)
        res[span, width:] = mt(proj_in[span, :], wi_ref[...]).astype(BF)
        return carry

    lax.fori_loop(0, cities * IN_MAX // 512, gather_step, 0)
    lax.fori_loop(0, cities, in_step, 0, unroll=4)
    lax.fori_loop(0, cities * IN_MAX // 512, pull_step, 0)

    slots = cities * IN_MAX

    def put_back(dst, begin, count):
        pick = onehot(flat_col[begin : begin + count, 0:1], iota((count, slots), 1))
        dst[begin : begin + count, :] = mm(pick, res[...]).astype(BF)

    put_back(ret, edge, cities * CROSS)
    home_copies[0].start()
    for s in range(1, n_arc):
        put_back(ret, s * slot, slot)
        home_copies[s].start()
    put_back(back, 0, slot)
    lax.fori_loop(pairs // 2, pairs, out_step, 0, unroll=2)
    for c in home_copies:
        c.wait()

    perm = onehot(place(iota((block, 1), 0)), iota((block, block), 1))
    for g in range(cities // group):
        moved = [back[pl.ds(s * slot + g * g_slot, g_slot), :] for s in range(n_arc)]
        moved.append(back[pl.ds(edge + g * g_edge, g_edge), :])
        home = mm(perm, jnp.concatenate(moved, axis=0))
        span = pl.ds(g * block, block)
        mixed_ref[span, :] = (
            mix_part[span, :] + mm(home[:, :width].astype(BF), wm[width:])
        ).astype(BF)
        grad_ref[span, :] = (grad_part[span, :] + home[:, width:]).astype(BF)


def body(features, cotangent, w_out_att, w_in_att, w_mix, in_degree, in_order):
    cities, arcs, width = features.shape[2:]
    rows = cities * arcs
    n_arc = lax.axis_size("arc")
    n_clu = lax.axis_size("clu")
    per = INNER // n_arc
    group = next(g for g in (4, 8, 16) if (g * per) % 16 == 0)
    vmem = pl.BlockSpec(memory_space=pltpu.VMEM)
    smem = pl.BlockSpec(memory_space=pltpu.SMEM)
    copies = 2 * (n_arc + 1)
    mixed, grad = pl.pallas_call(
        functools.partial(kernel, n_arc, n_clu, group),
        out_shape=[jax.ShapeDtypeStruct((rows, width), BF)] * 2,
        in_specs=[smem] + [pl.BlockSpec(memory_space=pltpu.HBM)] * 5 + [vmem],
        out_specs=[vmem, vmem],
        scratch_shapes=[
            pltpu.VMEM((rows, width), BF),
            pltpu.VMEM((rows, width), BF),
            pltpu.VMEM(w_out_att.shape, BF),
            pltpu.VMEM(w_in_att.shape, BF),
            pltpu.VMEM(w_mix.shape, BF),
            pltpu.VMEM((cities * IN_MAX, 3 * width), BF),
            pltpu.VMEM((cities * IN_MAX, width), BF),
            pltpu.VMEM((rows, 2 * width), BF),
            pltpu.VMEM((rows, 2 * width), BF),
            pltpu.VMEM((rows, 2 * width), BF),
            pltpu.VMEM((rows, 2 * width), BF),
            pltpu.VMEM((cities * IN_MAX, 2 * width), BF),
            pltpu.VMEM((rows, width), F32),
            pltpu.VMEM((rows, width), F32),
            pltpu.VMEM((8, rows), F32),
            pltpu.VMEM((rows, 128), F32),
            pltpu.SemaphoreType.DMA((copies,)),
            pltpu.SemaphoreType.DMA((copies,)),
            pltpu.SemaphoreType.DMA((5,)),
        ],
        compiler_params=pltpu.CompilerParams(
            collective_id=0, has_side_effects=True, vmem_limit_bytes=63*1024*1024
        ),
    )(
        in_degree.reshape(cities),
        features.reshape(rows, width),
        cotangent.reshape(rows, width),
        w_out_att,
        w_in_att,
        w_mix,
        in_order.reshape(1, rows),
    )
    return mixed.reshape(features.shape), grad.reshape(features.shape)


def solution(mesh):
    in_specs = (
        P(("grp", "clu"), "arc", None, None, None),
        P(("grp", "clu"), "arc", None, None, None),
        P(),
        P(),
        P(),
        P(("grp", "clu"), "arc", None),
        P(("grp", "clu"), "arc", None),
    )
    out_specs = (
        P(("grp", "clu"), "arc", None, None, None),
        P(("grp", "clu"), "arc", None, None, None),
    )
    return jax.shard_map(body, mesh=mesh, in_specs=in_specs, out_specs=out_specs, check_vma=False)
```
